32 devices in a mesh: thick: 4 (over y, core), wide: 8 (over z, x).
Axes of the slice: x: 2, y: 2, z: 4, core: 2. Of those that a mesh axis runs over, the one named last changes fastest.
Arguments:
- phase_in: float32 [128, 512, 512], P('thick', 'wide'), may hold values from -1 to 1
- density_in: float32 [128, 512, 512], P('thick', 'wide'), may hold values from 0 to 1
Outputs:
- phase_out: float32 [128, 512, 512], P('thick', 'wide')
- density_out: float32 [128, 512, 512], P('thick', 'wide')
- mean_flux: float32 [], replicated
The draws below stay inside these ranges and needn't reach their ends.
All inputs are finite; a program needn't handle non-finite values.
Results may differ from the reference program's by a relative error of at most 0.0001.
Values sent between devices are 32-bit elements; how exact they have to be, the bound alone decides.
A program may use at most 192 MiB of HBM per device.

```python
import math
import jax
import jax.numpy as jnp

NX = 512
NY = 512
NZ = 128
CH_STEPS = 1
DIFF_STEPS = 3


def level_of(rng, dims, cuts, smallest, largest):
    gain = 1.0
    for position, parts in cuts:
        steps = jax.random.uniform(jax.random.fold_in(jax.random.fold_in(rng, 6), position), (parts,), jnp.float32, smallest / len(cuts), largest / len(cuts))
        gain = gain * jnp.repeat(jnp.exp(steps), dims[position] // parts).reshape((-1,) + (1,) * (len(dims) - 1 - position))
    return gain


def setup_inputs(seed: int = 0) -> dict:
    keys = jax.random.split(jax.random.key(seed), 3)
    phase_in = jnp.clip(jax.random.uniform(keys[0], (NZ, NX, NY), jnp.float32, -1.0, 1.0) * level_of(keys[0], (NZ, NX, NY), ((0, 4), (1, 8)), -0.4, 0.0), -1.0, 1.0)
    density_in = jnp.clip(1.0 * jax.random.uniform(keys[1], (NZ, NX, NY), jnp.float32) ** level_of(keys[1], (NZ, NX, NY), ((0, 4), (1, 8)), -0.2, 0.2), 0.0, 1.0)
    return dict(phase_in=phase_in, density_in=density_in)


time_step = 100.0
stabilizer = 3.0
gradient_energy = 2.0
walk_step = 0.16


def squared(length):
    return (2.0 * math.pi * jnp.fft.fftfreq(length)) ** 2


def spectral_step(phase):
    wave = squared(NZ)[:, None, None] + squared(NX)[None, :, None] + squared(NY)[None, None, :]
    chemical = phase * phase * phase - phase
    spectrum = ((1.0 + time_step * stabilizer * wave) * jnp.fft.fftn(phase) - time_step * wave * jnp.fft.fftn(chemical))
    spectrum = spectrum / (1.0 + time_step * stabilizer * wave + time_step * gradient_energy * wave * wave)
    return jnp.real(jnp.fft.ifftn(spectrum)).astype(phase.dtype)


def advance(density, conduct):
    centre = density[1:-1, 1:-1]
    middle = conduct[1:-1, 1:-1]

    def inflow(near_density, near_conduct):
        return 0.5 * (near_conduct + middle) * (near_density - centre)

    lower = inflow(density[:-2, 1:-1], conduct[:-2, 1:-1])
    total = lower + inflow(density[2:, 1:-1], conduct[2:, 1:-1])
    total = total + inflow(density[1:-1, :-2], conduct[1:-1, :-2]) + inflow(density[1:-1, 2:], conduct[1:-1, 2:])
    total = total + inflow(jnp.roll(centre, 1, 2), jnp.roll(middle, 1, 2)) + inflow(jnp.roll(centre, -1, 2), jnp.roll(middle, -1, 2))
    return centre + walk_step * total, lower


def wrap_rows(field):
    return jnp.concatenate([field[:, -1:], field, field[:, :1]], 1)


def reference(phase_in, density_in):
    phase = phase_in
    for turn in range(CH_STEPS):
        phase = spectral_step(phase)
    conduct = 0.05 + 0.95 * jax.nn.sigmoid(4.0 * phase)
    conduct_ext = wrap_rows(jnp.concatenate([conduct[:1], conduct, conduct[-1:]], 0))
    density = density_in
    lower = jnp.zeros_like(density)
    for turn in range(DIFF_STEPS):
        bottom = jnp.ones((1, NX, NY), density.dtype)
        upper = jnp.zeros((1, NX, NY), density.dtype)
        padded = wrap_rows(jnp.concatenate([bottom, density, upper], 0))
        density, lower = advance(padded, conduct_ext)
    flux = jnp.sum(lower) / (NX * NY)
    return phase, density, flux
```

```python
import math

import jax
import jax.numpy as jnp
from jax import lax
from jax.sharding import PartitionSpec as P

NX = 512
NY = 512
NZ = 128
DIFF_STEPS = 3


time_step = 100.0
stabilizer = 3.0
gradient_energy = 2.0
walk_step = 0.16


def with_halo(array, sides, width):
    for axis, dim in sides:
        peers, length = (lax.axis_size(axis), array.shape[dim])
        up = [(i, (i + 1) % peers) for i in range(peers)]
        down = [(j, i) for i, j in up]
        last = lax.slice_in_dim(array, length - width, length, axis=dim)
        leading = lax.slice_in_dim(array, 0, width, axis=dim)
        before = lax.ppermute(last, axis, up)
        after = lax.ppermute(leading, axis, down)
        array = jnp.concatenate([before, array, after], axis=dim)
    return array


def hartley(length):
    index = jnp.arange(length, dtype=jnp.int32)
    folded = index[:, None] * index[None, :] % length
    angle = folded.astype(jnp.float32) * (2.0 * math.pi / length)
    return jnp.cos(angle) + jnp.sin(angle)


def squared_wave(index, length):
    signed = jnp.where(index < length // 2, index, index - length).astype(jnp.float32)
    return (signed * (2.0 * math.pi / length)) ** 2


def product(form, left, right):
    return jnp.einsum(form, left, right, precision=lax.Precision.HIGH)


def advance(density, conduct):
    centre = density[1:-1, 1:-1]
    middle = conduct[1:-1, 1:-1]

    def inflow(near_density, near_conduct):
        return 0.5 * (near_conduct + middle) * (near_density - centre)

    lower = inflow(density[:-2, 1:-1], conduct[:-2, 1:-1])
    total = lower + inflow(density[2:, 1:-1], conduct[2:, 1:-1])
    total = (
        total
        + inflow(density[1:-1, :-2], conduct[1:-1, :-2])
        + inflow(density[1:-1, 2:], conduct[1:-1, 2:])
    )
    total = (
        total
        + inflow(jnp.roll(centre, 1, 2), jnp.roll(middle, 1, 2))
        + inflow(jnp.roll(centre, -1, 2), jnp.roll(middle, -1, 2))
    )
    return (centre + walk_step * total, lower)


def total_over(value, axis):
    peers = lax.axis_size(axis)
    if peers & (peers - 1):
        return lax.psum(value, axis)
    step = 1
    while step < peers:
        value = value + lax.ppermute(value, axis, [(i, i ^ step) for i in range(peers)])
        step *= 2
    return value


def exchange(array, axis):
    return lax.all_to_all(array, axis, split_axis=0, concat_axis=0, tiled=True)


def evolve(phase):
    wides = lax.axis_size("wide")
    thicks = lax.axis_size("thick")
    depth, rows, _ = phase.shape
    y_share = NY // wides
    x_share = NX // thicks
    matrix_y = hartley(NY)
    matrix_x = hartley(NX)
    matrix_z = hartley(NZ)
    wave_y = squared_wave(
        lax.axis_index("wide") * y_share + jnp.arange(y_share, dtype=jnp.int32), NY
    )
    wave_x = squared_wave(
        lax.axis_index("thick") * x_share + jnp.arange(x_share, dtype=jnp.int32), NX
    )
    wave_z = squared_wave(jnp.arange(NZ, dtype=jnp.int32), NZ)
    wave = wave_x[:, None, None] + wave_z[None, :, None] + wave_y[None, None, :]
    implicit = 1.0 + time_step * stabilizer * wave + time_step * gradient_energy * wave * wave
    factor = 1.0 / (NX * NY * NZ)
    keep = (1.0 + time_step * stabilizer * wave) / implicit * factor
    drive = -time_step * wave / implicit * factor

    chemical = phase * phase * phase - phase
    fields = jnp.stack([phase, chemical])
    part = product("fzxy,ywk->wzxfk", fields, matrix_y.reshape(NY, wides, y_share))
    part = exchange(part.reshape(wides, depth, rows, 2 * y_share), "wide")
    split_x = matrix_x.reshape(wides, rows, thicks, x_share)
    part = exchange(product("wzxc,wxtk->tkzc", part, split_x), "thick")
    split_z = matrix_z.reshape(thicks, depth, NZ)
    part = product("tkzc,tzm->kmc", part, split_z)
    part = keep * part[:, :, :y_share] + drive * part[:, :, y_share:]
    part = part.reshape(2, x_share // 2, NZ, y_share)
    part = product("pkmc,tzm->tkzpc", part, split_z)
    part = exchange(part.reshape(thicks, x_share // 2, depth, 2 * y_share), "thick")
    part = part.reshape(thicks, x_share // 2, 2, depth // 2, 2, y_share)
    back_x = matrix_x.reshape(thicks, 2, x_share // 2, wides, rows)
    part = product("tkqzpc,tpkwx->wzxqc", part, back_x)
    part = exchange(part.reshape(wides, depth // 2, rows, 2 * y_share), "wide")
    part = part.reshape(wides, depth // 2, rows, 2, y_share)
    part = product("wzxqc,wcy->qzxy", part, matrix_y.reshape(wides, y_share, NY))
    return part.reshape(depth, rows, NY)


def per_device(phase_in, density_in):
    position = lax.axis_index("thick")
    final = lax.axis_size("thick") - 1
    sides = (("thick", 0), ("wide", 1))
    density = with_halo(density_in, sides, DIFF_STEPS)
    phase = evolve(phase_in)
    conduct = with_halo(0.05 + 0.95 * jax.nn.sigmoid(4.0 * phase), sides, DIFF_STEPS)
    depth = conduct.shape[0]
    layer = jnp.arange(depth, dtype=jnp.int32)[:, None, None]
    first = conduct[DIFF_STEPS : DIFF_STEPS + 1]
    last = conduct[depth - DIFF_STEPS - 1 : depth - DIFF_STEPS]
    conduct = jnp.where((position == 0) & (layer < DIFF_STEPS), first, conduct)
    conduct = jnp.where((position == final) & (layer >= depth - DIFF_STEPS), last, conduct)
    lower = jnp.zeros_like(density_in)
    for turn in range(DIFF_STEPS):
        margin = DIFF_STEPS - turn
        if turn:
            conduct = conduct[1:-1, 1:-1]
        depth = density.shape[0]
        layer = jnp.arange(depth, dtype=jnp.int32)[:, None, None]
        density = jnp.where((position == 0) & (layer < margin), 1.0, density)
        density = jnp.where((position == final) & (layer >= depth - margin), 0.0, density)
        density, lower = advance(density, conduct)
    flux = total_over(total_over(jnp.sum(lower), "thick"), "wide") / (NX * NY)
    return (phase, density, flux)


def solution(mesh):
    in_specs = (P("thick", "wide", None), P("thick", "wide", None))
    out_specs = (P("thick", "wide", None), P("thick", "wide", None), P())
    return jax.shard_map(
        per_device, mesh=mesh, in_specs=in_specs, out_specs=out_specs, check_vma=False
    )
```

```python
import math

import jax
import jax.numpy as jnp
from jax import lax
from jax.sharding import PartitionSpec as P

NX = 512
NY = 512
NZ = 128
DIFF_STEPS = 3
CHUNKS = 2


time_step = 100.0
stabilizer = 3.0
gradient_energy = 2.0
walk_step = 0.16


def with_halo(array, sides, width):
    for axis, dim in sides:
        peers, length = (lax.axis_size(axis), array.shape[dim])
        up = [(i, (i + 1) % peers) for i in range(peers)]
        down = [(j, i) for i, j in up]
        last = lax.slice_in_dim(array, length - width, length, axis=dim)
        leading = lax.slice_in_dim(array, 0, width, axis=dim)
        before = lax.ppermute(last, axis, up)
        after = lax.ppermute(leading, axis, down)
        array = jnp.concatenate([before, array, after], axis=dim)
    return array


def hartley(length):
    index = jnp.arange(length, dtype=jnp.int32)
    folded = index[:, None] * index[None, :] % length
    angle = folded.astype(jnp.float32) * (2.0 * math.pi / length)
    return jnp.cos(angle) + jnp.sin(angle)


def squared_wave(index, length):
    signed = jnp.where(index < length // 2, index, index - length).astype(jnp.float32)
    return (signed * (2.0 * math.pi / length)) ** 2


def product(form, left, right):
    return jnp.einsum(form, left, right, precision=lax.Precision.HIGH)


def advance(density, conduct):
    centre = density[1:-1, 1:-1]
    middle = conduct[1:-1, 1:-1]

    def inflow(near_density, near_conduct):
        return 0.5 * (near_conduct + middle) * (near_density - centre)

    lower = inflow(density[:-2, 1:-1], conduct[:-2, 1:-1])
    total = lower + inflow(density[2:, 1:-1], conduct[2:, 1:-1])
    total = (
        total
        + inflow(density[1:-1, :-2], conduct[1:-1, :-2])
        + inflow(density[1:-1, 2:], conduct[1:-1, 2:])
    )
    total = (
        total
        + inflow(jnp.roll(centre, 1, 2), jnp.roll(middle, 1, 2))
        + inflow(jnp.roll(centre, -1, 2), jnp.roll(middle, -1, 2))
    )
    return (centre + walk_step * total, lower)


def total_over(value, axis):
    peers = lax.axis_size(axis)
    if peers & (peers - 1):
        return lax.psum(value, axis)
    step = 1
    while step < peers:
        value = value + lax.ppermute(value, axis, [(i, i ^ step) for i in range(peers)])
        step *= 2
    return value


def exchange(array, axis):
    return lax.all_to_all(array, axis, split_axis=0, concat_axis=0, tiled=True)


def evolve(phase):
    wides = lax.axis_size("wide")
    thicks = lax.axis_size("thick")
    depth, rows, _ = phase.shape
    y_share = NY // wides
    x_share = NX // thicks
    matrix_y = hartley(NY)
    matrix_x = hartley(NX)
    matrix_z = hartley(NZ)
    wave_y = squared_wave(
        lax.axis_index("wide") * y_share + jnp.arange(y_share, dtype=jnp.int32), NY
    )
    wave_x = squared_wave(
        lax.axis_index("thick") * x_share + jnp.arange(x_share, dtype=jnp.int32), NX
    )
    wave_z = squared_wave(jnp.arange(NZ, dtype=jnp.int32), NZ)
    wave = wave_x[:, None, None] + wave_z[None, :, None] + wave_y[None, None, :]
    implicit = 1.0 + time_step * stabilizer * wave + time_step * gradient_energy * wave * wave
    factor = 1.0 / (NX * NY * NZ)
    keep = (1.0 + time_step * stabilizer * wave) / implicit * factor
    drive = -time_step * wave / implicit * factor

    chemical = phase * phase * phase - phase
    fields = jnp.concatenate([phase, chemical], axis=2)
    split_y = matrix_y.reshape(NY, wides, y_share)
    empty = jnp.zeros_like(split_y)
    forward_y = jnp.concatenate(
        [jnp.concatenate([split_y, empty], axis=2), jnp.concatenate([empty, split_y], axis=2)],
        axis=0,
    )
    forward_x = matrix_x.reshape(wides, rows, thicks, x_share)
    split_z = matrix_z.reshape(thicks, depth, NZ)
    back_x = matrix_x.reshape(thicks, 2, x_share // 2, wides, rows)
    split_y = matrix_y.reshape(wides, y_share, NY)
    empty = jnp.zeros_like(split_y)
    back_y = jnp.stack(
        [
            jnp.concatenate([split_y, empty], axis=1),
            jnp.concatenate([empty, split_y], axis=1),
        ]
    )
    share = depth // CHUNKS
    spectrum = 0.0
    for chunk in range(CHUNKS):
        layers = slice(chunk * share, (chunk + 1) * share)
        part = product("zxy,ywk->wzxk", fields[layers], forward_y)
        part = exchange(part, "wide")
        part = exchange(product("wzxc,wxtk->tkzc", part, forward_x), "thick")
        spectrum = spectrum + product("tkzc,tzm->kmc", part, split_z[:, layers])
    spectrum = keep * spectrum[:, :, :y_share] + drive * spectrum[:, :, y_share:]
    half = x_share // 2
    spectrum = jnp.concatenate([spectrum[:half], spectrum[half:]], axis=2)
    pieces = []
    for chunk in range(CHUNKS):
        layers = slice(chunk * share, (chunk + 1) * share)
        part = exchange(product("kmc,tzm->tkzc", spectrum, split_z[:, layers]), "thick")
        part = product("tkzc,tpkwx->pwzxc", part, back_x)
        part = part[0, ..., :y_share] + part[1, ..., y_share:]
        part = jnp.concatenate([part[:, : share // 2], part[:, share // 2 :]], axis=3)
        part = exchange(part, "wide")
        part = product("wzxc,qwcy->qzxy", part, back_y)
        pieces.append(part.reshape(share, rows, NY))
    return jnp.concatenate(pieces, axis=0)


def per_device(phase_in, density_in):
    position = lax.axis_index("thick")
    final = lax.axis_size("thick") - 1
    sides = (("thick", 0), ("wide", 1))
    density = with_halo(density_in, sides, DIFF_STEPS)
    phase = evolve(phase_in)
    conduct = with_halo(0.05 + 0.95 * jax.nn.sigmoid(4.0 * phase), sides, DIFF_STEPS)
    depth = conduct.shape[0]
    layer = jnp.arange(depth, dtype=jnp.int32)[:, None, None]
    first = conduct[DIFF_STEPS : DIFF_STEPS + 1]
    last = conduct[depth - DIFF_STEPS - 1 : depth - DIFF_STEPS]
    conduct = jnp.where((position == 0) & (layer < DIFF_STEPS), first, conduct)
    conduct = jnp.where((position == final) & (layer >= depth - DIFF_STEPS), last, conduct)
    lower = jnp.zeros_like(density_in)
    for turn in range(DIFF_STEPS):
        margin = DIFF_STEPS - turn
        if turn:
            conduct = conduct[1:-1, 1:-1]
        depth = density.shape[0]
        layer = jnp.arange(depth, dtype=jnp.int32)[:, None, None]
        density = jnp.where((position == 0) & (layer < margin), 1.0, density)
        density = jnp.where((position == final) & (layer >= depth - margin), 0.0, density)
        density, lower = advance(density, conduct)
    flux = total_over(total_over(jnp.sum(lower), "thick"), "wide") / (NX * NY)
    return (phase, density, flux)


def solution(mesh):
    in_specs = (P("thick", "wide", None), P("thick", "wide", None))
    out_specs = (P("thick", "wide", None), P("thick", "wide", None), P())
    return jax.shard_map(
        per_device, mesh=mesh, in_specs=in_specs, out_specs=out_specs, check_vma=False
    )
```
